256 devices in a mesh: ka: 16 (over z_hi, x, core), vert: 16 (over y, z_lo).
Axes of the slice: x: 4, y: 4, z: 8 (z_hi: 2, z_lo: 4; z = z_hi * 4 + z_lo), core: 2. Of those that a mesh axis runs over, the one named last changes fastest.
Arguments:
- amplitudes: bfloat16 [1, 16, 16, 16, 96, 1536], P(None, 'ka', None, None, 'vert'), may hold values from -12 to 12
- loop_integral_blocks: bfloat16 [16, 1536, 1536], P('ka', 'vert'), may hold values from -0.15625 to 0.15625
- occupied_energy: float32 [16, 16], replicated, may hold values from -2 to -0.5
- occupied_energy_j: float32 [1, 16], replicated, may hold values from -2 to -0.5
- virtual_energy: float32 [16, 96], replicated, may hold values from 0.5 to 2.5
- kpoint_b_table: int32 [1, 16, 16], replicated, may hold values from 0 to 15, as said below
Outputs:
- update: bfloat16 [1, 16, 16, 16, 96, 1536], P(None, 'ka', None, None, 'vert')
The draws below stay inside these ranges and needn't reach their ends.
Inputs may be any that keep to these rules, and one draw needn't show every extreme that they name: For every kj and ki, kpoint_b_table[kj, ki, :] is a permutation of the 16 k-points.
All inputs are finite; a program needn't handle non-finite values.
Results may differ from the reference program's by a relative error of at most 0.0051.
Values may be sent and summed in bfloat16 or wider, within the bound.
No kernel may reach another device: no remote copies, remote signals or barrier semaphores. Data moves between devices by JAX's collectives and lax.ppermute only.
A program may use at most 128 MiB of HBM per device.

```python
import jax
import jax.numpy as jnp
from jax import lax

OCC_ORBITALS = 16
VIRT_ORBITALS = 96
KJW = 1
NK = 16


def draw_kpoint_b_table(key, part):
    key = jax.random.fold_in(key, 5)
    row_keys = jax.random.split(key, KJW * NK)
    base = jnp.arange(NK, dtype=jnp.int32)
    rows = jax.vmap(lambda row_key: jax.random.permutation(row_key, base))(row_keys)
    return rows.reshape(KJW, NK, NK).astype(jnp.int32)


def level_of(own_key, dims, cuts, smallest, high):
    factor_of, own = 1.0, jax.random.fold_in(own_key, 6)
    for axis_at, parts in cuts:
        steps = jnp.exp(jax.random.uniform(jax.random.fold_in(own, axis_at), (parts,), jnp.float32, smallest / len(cuts), high / len(cuts)))
        factor_of = factor_of * jnp.repeat(steps, dims[axis_at] // parts).reshape([-1 if axis == axis_at else 1 for axis in range(len(dims))])
    return factor_of


def centred(own_key, dims, width, limit, shards=(), kind=jnp.bfloat16):
    values = width * jax.random.normal(own_key, dims, jnp.float32)
    if shards:
        values = values * level_of(own_key, dims, shards, -0.22, 0.18)
    return jnp.clip(values, -limit, limit).astype(kind)


def setup_inputs(seed: int = 0) -> dict:
    streams_of = jax.random.split(jax.random.key(seed), 7)
    return {
        "amplitudes": centred(streams_of[0], (KJW, NK, NK, OCC_ORBITALS, VIRT_ORBITALS, OCC_ORBITALS * VIRT_ORBITALS), 2.0, 12.0, ((1, 16), (4, 16))),
        "loop_integral_blocks": centred(streams_of[1], (NK, OCC_ORBITALS * VIRT_ORBITALS, OCC_ORBITALS * VIRT_ORBITALS), (OCC_ORBITALS * VIRT_ORBITALS) ** -0.5, 0.15625, ((0, 16), (1, 16))),
        "occupied_energy": jnp.clip(jax.random.uniform(streams_of[2], (NK, OCC_ORBITALS), jnp.float32, -2.0, -0.5), -2.0, -0.5),
        "occupied_energy_j": jnp.clip(jax.random.uniform(streams_of[3], (KJW, OCC_ORBITALS), jnp.float32, -2.0, -0.5), -2.0, -0.5),
        "virtual_energy": jnp.clip(jax.random.uniform(streams_of[4], (NK, VIRT_ORBITALS), jnp.float32, 0.5, 2.5), 0.5, 2.5),
        "kpoint_b_table": draw_kpoint_b_table(jax.random.fold_in(streams_of[6], 71), 0),
    }


def reference(amplitudes, loop_integral_blocks, occupied_energy, occupied_energy_j, virtual_energy, kpoint_b_table):
    blocks = amplitudes.astype(jnp.float32).reshape(KJW, NK, NK, OCC_ORBITALS, VIRT_ORBITALS, OCC_ORBITALS, VIRT_ORBITALS)
    swapped = jnp.swapaxes(blocks, 3, 5)
    joined_terms = (2.0 * blocks - swapped).astype(jnp.bfloat16).reshape(KJW, NK, NK, OCC_ORBITALS * VIRT_ORBITALS, OCC_ORBITALS * VIRT_ORBITALS)
    virtual_b = virtual_energy[kpoint_b_table]

    def single_block(kpoint_index):
        block_rows = joined_terms[:, :, kpoint_index].reshape(-1, OCC_ORBITALS * VIRT_ORBITALS)
        contracted_result = jnp.dot(block_rows, loop_integral_blocks[kpoint_index], preferred_element_type=jnp.float32)
        contracted_result = contracted_result.reshape(KJW, NK, OCC_ORBITALS, VIRT_ORBITALS, OCC_ORBITALS, VIRT_ORBITALS)
        energy_gap = (occupied_energy[None, :, :, None, None, None]
                 + occupied_energy_j[:, None, None, None, :, None]
                 - virtual_energy[kpoint_index][None, None, None, :, None, None]
                 - virtual_b[:, :, kpoint_index][:, :, None, None, None, :])
        return (contracted_result / energy_gap).astype(jnp.bfloat16).reshape(KJW, NK, OCC_ORBITALS, VIRT_ORBITALS, OCC_ORBITALS * VIRT_ORBITALS)

    result = lax.map(single_block, jnp.arange(NK, dtype=jnp.int32))
    return jnp.transpose(result, (1, 2, 0, 3, 4, 5))
```

```python
import jax
import jax.numpy as jnp
from jax import lax
from jax.experimental import pallas as pl
from jax.experimental.pallas import tpu as pltpu
from jax.sharding import Mesh, PartitionSpec as P

NO = 16
NV = 96
PAIRS = NO * NV
VS = 6
ROWS = VS * NO
HALF = NV // 2
VMEM = 48 << 20
RING = ("zh", "zl")


def combine_kernel(x_ref, o_ref, scr):
    sq = NO * NO
    for a in range(VS):
        xa = x_ref[0, NO * a : NO * a + NO, :].astype(jnp.float32)
        for p in range(NO):
            scr[a * sq + NO * p : a * sq + NO * p + NO, 0:NV] = xa[:, NV * p : NV * p + NV]
    for a in range(VS):
        xa = x_ref[0, NO * a : NO * a + NO, :].astype(jnp.float32)
        swapped = jnp.concatenate(
            [scr[pl.ds(a * sq + q, NO, stride=NO), :][:, :NV] for q in range(NO)], axis=1
        )
        o_ref[0, NO * a : NO * a + NO, :] = (2.0 * xa - swapped).astype(jnp.bfloat16)


def combine(x):
    nb = x.shape[0]
    spec = pl.BlockSpec((1, ROWS, PAIRS), lambda b: (b, 0, 0))
    return pl.pallas_call(
        combine_kernel,
        grid=(nb,),
        in_specs=[spec],
        out_specs=spec,
        out_shape=jax.ShapeDtypeStruct(x.shape, x.dtype),
        scratch_shapes=[pltpu.VMEM((VS * NO * NO, 128), jnp.float32)],
        compiler_params=pltpu.CompilerParams(vmem_limit_bytes=VMEM),
        cost_estimate=pl.CostEstimate(
            flops=nb * 300000000, bytes_accessed=4 * x.size, transcendentals=0
        ),
        name="combine",
    )(x)


NT = 256


def contract(cs, w, rr, cc):
    nc = len(cs)

    def kernel(*refs):
        x_refs, (w_ref, r_ref, c_ref), o_refs = refs[:nc], refs[nc : nc + 3], refs[nc + 3 :]
        x = jnp.concatenate([ref[0] for ref in x_refs], axis=0) if nc > 1 else x_refs[0][0]
        acc = jnp.dot(x, w_ref[0], preferred_element_type=jnp.float32)
        for m in range(nc):
            gap = r_ref[0, m] + c_ref[0, m]
            o_refs[m][0] = (acc[ROWS * m : ROWS * m + ROWS] / gap).astype(jnp.bfloat16)

    row = pl.BlockSpec((1, ROWS, PAIRS), lambda z, n: (z, 0, 0))
    return pl.pallas_call(
        kernel,
        grid=(2, PAIRS // NT),
        in_specs=[row] * nc
        + [
            pl.BlockSpec((1, PAIRS, NT), lambda z, n: (z, 0, n)),
            pl.BlockSpec((1, nc, ROWS, 1), lambda z, n: (z, 0, 0, 0)),
            pl.BlockSpec((1, nc, 1, NT), lambda z, n: (z, 0, 0, n)),
        ],
        out_specs=[pl.BlockSpec((1, ROWS, NT), lambda z, n: (z, 0, n))] * nc,
        out_shape=[jax.ShapeDtypeStruct((2, ROWS, PAIRS), jnp.bfloat16)] * nc,
        compiler_params=pltpu.CompilerParams(vmem_limit_bytes=VMEM),
        cost_estimate=pl.CostEstimate(
            flops=2 * 2 * nc * ROWS * PAIRS * PAIRS, bytes_accessed=4 * PAIRS * PAIRS, transcendentals=0
        ),
        name="contract",
    )(*cs, w, rr, cc)


def assemble(ring, gathered, pos):
    n = len(ring)

    def kernel(pos_ref, *refs):
        pieces, g_ref, o_ref, sem = refs[:n], refs[n], refs[n + 1], refs[n + 2]
        y, z = pos_ref[0], pos_ref[1]
        copies = []
        for s in range(n):
            src = lax.rem(z + s, n)
            for d in range(4):
                copies.append(
                    pltpu.make_async_copy(
                        pieces[s].at[d],
                        o_ref.at[lax.div(src, 4), lax.rem(y + d, 4), lax.rem(src, 4), 0],
                        sem.at[len(copies)],
                    )
                )
        for zh in range(2):
            for yy in range(4):
                for zl in range(4):
                    copies.append(
                        pltpu.make_async_copy(
                            g_ref.at[zh, zl, yy], o_ref.at[zh, yy, zl, 1], sem.at[len(copies)]
                        )
                    )
        for c in copies:
            c.start()
        for c in copies:
            c.wait()

    anyspec = pl.BlockSpec(memory_space=pl.ANY)
    return pl.pallas_call(
        kernel,
        in_specs=[pl.BlockSpec(memory_space=pltpu.SMEM)] + [anyspec] * (n + 1),
        out_specs=anyspec,
        out_shape=jax.ShapeDtypeStruct((2, 4, 4, 2, HALF, PAIRS), jnp.bfloat16),
        scratch_shapes=[pltpu.SemaphoreType.DMA((64,))],
        compiler_params=pltpu.CompilerParams(vmem_limit_bytes=4 << 20),
        cost_estimate=pl.CostEstimate(flops=0, bytes_accessed=8 * PAIRS * PAIRS, transcendentals=0),
        name="assemble",
    )(pos, *ring, gathered)


def xc_permute(v, dx, dc):
    if dx == 0:
        return lax.ppermute(v, "c", [(0, 1), (1, 0)])
    pairs = [
        (x * 2 + c, ((x + dx) % 4) * 2 + (c ^ dc)) for x in range(4) for c in range(2)
    ]
    return lax.ppermute(v, ("x", "c"), pairs)


def y_permute(v, s):
    return lax.ppermute(v, "y", [(i, (i + s) % 4) for i in range(4)])


def z_permute(v, s):
    return lax.ppermute(v, RING, [(i, (i + s) % 8) for i in range(8)])


CHUNKS = [(2, 0), (2, 1), (1, 0), (1, 1), (3, 0), (3, 1), (0, 1), (0, 0)]
GROUPS = [(0, 2), (2, 6), (6, 8)]


def per_device(amps, wshard, occ, occj, virt, table):
    zh, x, c = lax.axis_index("zh"), lax.axis_index("x"), lax.axis_index("c")
    y, zl = lax.axis_index("y"), lax.axis_index("zl")
    blocks = jnp.transpose(amps[0, 0], (0, 2, 1, 3)).reshape(2, 4, 2, ROWS, PAIRS)

    def block(dx, dc):
        return lax.dynamic_slice(
            blocks, (0, lax.rem(x + dx, 4), c ^ dc, 0, 0), (2, 1, 1, ROWS, PAIRS)
        ).reshape(2, ROWS, PAIRS)

    sent = [block(dx, dc) for dx, dc in CHUNKS]
    got = [
        v if (dx, dc) == (0, 0) else xc_permute(v, dx, dc) for v, (dx, dc) in zip(sent, CHUNKS)
    ]

    w = wshard[0]
    gathered = lax.all_gather(w[HALF:], ("zh", "zl", "y"), axis=0).reshape(2, 4, 4, HALF, PAIRS)
    own = w[:HALF]
    col = jnp.stack([own, y_permute(own, -1), y_permute(own, 2), y_permute(own, 1)])
    up, down = [col], [col]
    for s in range(3):
        up.append(z_permute(up[-1], 1))
        down.append(z_permute(down[-1], -1))
    far = jnp.concatenate([z_permute(up[3][:2], 1), z_permute(down[3][2:], -1)])
    ring = [col, down[1], down[2], down[3], far, up[3], up[2], up[1]]
    pos = jnp.stack([y, zh * 4 + zl]).astype(jnp.int32)
    wall = assemble(ring, gathered, pos).reshape(2, PAIRS, PAIRS)

    ki = jnp.stack([(zh * 4 + lax.rem(x + 4 - dx, 4)) * 2 + (c ^ dc) for dx, dc in CHUNKS])
    ka = jnp.stack([(z * 4 + x) * 2 + c for z in range(2)])
    va = lax.dynamic_slice(virt, (0, (y * 4 + zl) * VS), (NO, VS))[ka]
    rr = occ[ki][None, :, None, :] - va[:, None, :, None]
    rr = rr.reshape(2, len(CHUNKS), ROWS, 1)
    kb = table[0][ki][:, ka].T
    cc = occj[0][None, None, :, None] - virt[kb][:, :, None, :]
    cc = cc.reshape(2, len(CHUNKS), 1, PAIRS)

    out = jnp.zeros((2, 4, 2, ROWS, PAIRS), jnp.bfloat16)
    comb = [combine(v) for v in got]
    for lo, hi in GROUPS:
        res = contract(comb[lo:hi], wall, rr[:, lo:hi], cc[:, lo:hi])
        for v, (dx, dc) in zip(res, CHUNKS[lo:hi]):
            if (dx, dc) != (0, 0):
                v = xc_permute(v, (4 - dx) % 4, dc)
            out = lax.dynamic_update_slice(
                out, v.reshape(2, 1, 1, ROWS, PAIRS), (0, lax.rem(x + dx, 4), c ^ dc, 0, 0)
            )
    out = out.reshape(NO, VS, NO, PAIRS)
    return jnp.transpose(out, (0, 2, 1, 3))[None, None]


def solution(mesh):
    fine = Mesh(mesh.devices.reshape(2, 4, 2, 4, 4), ("zh", "x", "c", "y", "zl"))
    ka, vert = ("zh", "x", "c"), ("y", "zl")
    in_specs = (P(None, ka, None, None, vert, None), P(ka, vert, None), P(), P(), P(), P())
    out_specs = P(None, ka, None, None, vert, None)
    return jax.shard_map(
        per_device, mesh=fine, in_specs=in_specs, out_specs=out_specs, check_vma=False
    )
```

```python
import jax
import jax.numpy as jnp
from jax import lax
from jax.experimental import pallas as pl
from jax.experimental.pallas import tpu as pltpu
from jax.sharding import Mesh, PartitionSpec as P

NO = 16
NV = 96
PAIRS = NO * NV
VS = 6
ROWS = VS * NO
VMEM = 48 << 20
RING = ("zh", "zl")
NA = 768
NT = 384


def combine(x):
    nb, sq, step = x.shape[0], NO * NO, 4

    def kernel(x_ref, o_ref, scr):
        @pl.loop(0, step)
        def _(e):
            for a in range(VS):
                xa = x_ref[e, NO * a : NO * a + NO, :].astype(jnp.float32)
                for p in range(NO):
                    lo = a * sq + NO * p
                    scr[lo : lo + NO, 0:NV] = xa[:, NV * p : NV * p + NV]
            for a in range(VS):
                xa = x_ref[e, NO * a : NO * a + NO, :].astype(jnp.float32)
                swapped = jnp.concatenate(
                    [scr[pl.ds(a * sq + q, NO, stride=NO), :][:, :NV] for q in range(NO)], axis=1
                )
                o_ref[e, NO * a : NO * a + NO, :] = (2.0 * xa - swapped).astype(jnp.bfloat16)

    return pl.pallas_call(
        kernel,
        grid=(2, nb // step),
        in_specs=[pl.BlockSpec((step, None, ROWS, PAIRS), lambda q, b: (b, q, 0, 0))],
        out_specs=pl.BlockSpec((None, step, ROWS, PAIRS), lambda q, b: (q, b, 0, 0)),
        out_shape=jax.ShapeDtypeStruct((2, nb, ROWS, PAIRS), x.dtype),
        scratch_shapes=[pltpu.VMEM((VS * sq, 128), jnp.float32)],
        compiler_params=pltpu.CompilerParams(vmem_limit_bytes=VMEM),
        cost_estimate=pl.CostEstimate(
            flops=2 * nb * 300000000, bytes_accessed=4 * x.size, transcendentals=0
        ),
        name="combine",
    )(x)


def contract(comb, pos, pieces, place, rr, cc, lo, name):
    nb = comb.shape[1]
    width = NA if lo == 0 else PAIRS - NA
    npc = len(pieces)

    def kernel(pos_ref, x_ref, *refs):
        p_refs, (r_ref, c_ref, o_ref, w_ref) = refs[:npc], refs[npc:]
        q, n = pl.program_id(0), pl.program_id(1)

        @pl.when(n == 0)
        def _():
            place(p_refs, w_ref, q, pos_ref[0], pos_ref[1])

        cols = pl.ds(pl.multiple_of(n * NT, NT), NT)
        x = x_ref[...].reshape(nb * ROWS, PAIRS)
        acc = jnp.dot(x, w_ref[:, cols], preferred_element_type=jnp.float32)
        for m in range(nb):
            gap = r_ref[m] + c_ref[m]
            o_ref[m] = (acc[ROWS * m : ROWS * m + ROWS] / gap).astype(jnp.bfloat16)

    vmem = pl.BlockSpec(memory_space=pltpu.VMEM)
    return pl.pallas_call(
        kernel,
        grid=(2, width // NT),
        in_specs=[
            pl.BlockSpec(memory_space=pltpu.SMEM),
            pl.BlockSpec((None, nb, ROWS, PAIRS), lambda q, n: (q, 0, 0, 0)),
        ]
        + [vmem] * npc
        + [
            pl.BlockSpec((None, nb, ROWS, 1), lambda q, n: (q, 0, 0, 0)),
            pl.BlockSpec((None, nb, 1, NT), lambda q, n: (q, 0, 0, lo // NT + n)),
        ],
        out_specs=pl.BlockSpec((nb, None, ROWS, NT), lambda q, n: (0, q, 0, n)),
        out_shape=jax.ShapeDtypeStruct((nb, 2, ROWS, width), jnp.bfloat16),
        scratch_shapes=[pltpu.VMEM((PAIRS, width), jnp.bfloat16)],
        compiler_params=pltpu.CompilerParams(vmem_limit_bytes=VMEM),
        cost_estimate=pl.CostEstimate(
            flops=4 * nb * ROWS * PAIRS * width, bytes_accessed=8 * PAIRS * width, transcendentals=0
        ),
        name=name,
    )(pos, comb, *pieces, rr, cc)


def place_a(p_refs, w_ref, q, y, z):
    for zl in range(4):
        for e in range(4):
            k = lax.rem(y + e, 4) * 4 + zl
            w_ref[pl.ds(pl.multiple_of(k * NV, NV), NV), :] = p_refs[0][q * 4 + zl, e]


def place_b(p_refs, w_ref, q, y, z):
    for e in range(4):
        for zl in range(4):
            k = lax.rem(y + e, 4) * 4 + zl
            s = lax.rem(q * 4 + zl + 8 - z, 8)
            w_ref[pl.ds(pl.multiple_of(k * NV, NV), NV), :] = p_refs[e][s]


def merge(part, lo, out, name):
    nb, width = part.shape[0], part.shape[-1]

    def kernel(v_ref, *refs):
        refs[-1][...] = v_ref[...]

    return pl.pallas_call(
        kernel,
        grid=(2, nb // 4),
        in_specs=[pl.BlockSpec((4, None, ROWS, width), lambda q, b: (b, q, 0, 0))]
        + [pl.BlockSpec(memory_space=pl.ANY)] * (out is not None),
        out_specs=pl.BlockSpec((None, 4, ROWS, width), lambda q, b: (q, b, 0, lo // width)),
        out_shape=jax.ShapeDtypeStruct((2, nb, ROWS, PAIRS), jnp.bfloat16),
        input_output_aliases={} if out is None else {1: 0},
        compiler_params=pltpu.CompilerParams(vmem_limit_bytes=VMEM),
        name=name,
    )(part, *([] if out is None else [out]))


def y_permute(v, s):
    return lax.ppermute(v, "y", [(i, (i + s) % 4) for i in range(4)])


def z_permute(v, s):
    return lax.ppermute(v, RING, [(i, (i + s) % 8) for i in range(8)])


def tie(*vs):
    return lax.optimization_barrier(vs)


def gather_w(own, got):
    a, b = own[:, :NA], own[:, NA:]
    half = NV // 2
    a1, a2, a3 = y_permute(a, -1), y_permute(a, 2), y_permute(a, 1)
    up, down = [b], [b]
    for s in range(3):
        up.append(z_permute(up[-1], 1))
        down.append(z_permute(down[-1], -1))
        if s == 0:
            col = jnp.stack([a, a1, a2, a3])
            col, up[1], down[1] = tie(col, up[1], down[1])
    col = lax.all_gather(col, RING, axis=0)
    far = jnp.concatenate([z_permute(up[3][:half], 1), z_permute(down[3][half:], -1)])
    row = jnp.stack([b, down[1], down[2], down[3], far, up[3], up[2], up[1]])
    below, above = y_permute(row, 1), y_permute(row, -1)
    comb = combine(got)
    below, above, comb = tie(below, above, comb)
    far = jnp.concatenate([y_permute(below[:4], 1), y_permute(above[4:], -1)])
    return [col], [row, above, far, below], comb


def per_device(amps, wshard, occ, occj, virt, table):
    zh, x, c = lax.axis_index("zh"), lax.axis_index("x"), lax.axis_index("c")
    y, zl = lax.axis_index("y"), lax.axis_index("zl")
    pos = jnp.stack([y, zh * 4 + zl]).astype(jnp.int32)

    blocks = jnp.transpose(amps[0, 0], (0, 2, 1, 3)).reshape(2, 8, ROWS, PAIRS)
    blocks = jnp.swapaxes(blocks, 0, 1)
    own, blocks = tie(wshard[0], blocks)
    got = lax.all_to_all(blocks, ("x", "c"), split_axis=0, concat_axis=0, tiled=True)
    part_a, part_b, comb = gather_w(own, got)

    va = lax.dynamic_slice(virt, (0, (y * 4 + zl) * VS), (NO, VS)).reshape(2, 8, VS)
    va = lax.dynamic_index_in_dim(va, x * 2 + c, 1, False)
    occ_i = lax.dynamic_slice(occ, (zh * 8, 0), (8, NO))
    rr = (occ_i[None, :, None, :] - va[:, None, :, None]).reshape(2, 8, ROWS, 1)
    kb = lax.dynamic_slice(table[0], (zh * 8, 0), (8, NO)).reshape(8, 2, 8)
    kb = lax.dynamic_index_in_dim(kb, x * 2 + c, 2, False).T
    cc = (occj[0][None, None, :, None] - virt[kb][:, :, None, :]).reshape(2, 8, 1, PAIRS)

    out = None
    for lo, part, place, name in ((0, part_a, place_a, "_a"), (NA, part_b, place_b, "_b")):
        res = contract(comb, pos, part, place, rr, cc, lo, "contract" + name)
        res = lax.all_to_all(res, ("x", "c"), split_axis=0, concat_axis=0, tiled=True)
        out = merge(res, lo, out, "merge" + name)
    out = out.reshape(NO, VS, NO, PAIRS)
    return jnp.transpose(out, (0, 2, 1, 3))[None, None]


def solution(mesh):
    fine = Mesh(mesh.devices.reshape(2, 4, 2, 4, 4), ("zh", "x", "c", "y", "zl"))
    ka, vert = ("zh", "x", "c"), ("y", "zl")
    in_specs = (P(None, ka, None, None, vert, None), P(ka, vert, None), P(), P(), P(), P())
    out_specs = P(None, ka, None, None, vert, None)
    return jax.shard_map(
        per_device, mesh=fine, in_specs=in_specs, out_specs=out_specs, check_vma=False
    )
```

```python
import jax
import jax.numpy as jnp
from jax import lax
from jax.experimental import pallas as pl
from jax.experimental.pallas import tpu as pltpu
from jax.sharding import Mesh, PartitionSpec as P

NO = 16
NV = 96
PAIRS = NO * NV
VS = 6
ROWS = VS * NO
VMEM = 48 << 20
RING = ("zh", "zl")
NA = 384


def combine(x, q, out):
    nb, sq, step = x.shape[1], NO * NO, 2

    def kernel(x_ref, *refs):
        o_ref, scr = refs[-2:]

        @pl.loop(0, step)
        def _(e):
            for a in range(VS):
                xa = x_ref[e, NO * a : NO * a + NO, :].astype(jnp.float32)
                for p in range(NO):
                    lo = a * sq + NO * p
                    scr[lo : lo + NO, 0:NV] = xa[:, NV * p : NV * p + NV]
            for a in range(VS):
                xa = x_ref[e, NO * a : NO * a + NO, :].astype(jnp.float32)
                swapped = jnp.concatenate(
                    [scr[pl.ds(a * sq + q, NO, stride=NO), :][:, :NV] for q in range(NO)], axis=1
                )
                o_ref[e, NO * a : NO * a + NO, :] = (2.0 * xa - swapped).astype(jnp.bfloat16)

    return pl.pallas_call(
        kernel,
        grid=(nb // step,),
        in_specs=[pl.BlockSpec((None, step, ROWS, PAIRS), lambda b: (q, b, 0, 0))]
        + [pl.BlockSpec(memory_space=pl.ANY)] * (out is not None),
        out_specs=pl.BlockSpec((step, None, ROWS, PAIRS), lambda b: (b, q, 0, 0)),
        out_shape=jax.ShapeDtypeStruct((nb, 2, ROWS, PAIRS), x.dtype),
        input_output_aliases={} if out is None else {1: 0},
        scratch_shapes=[pltpu.VMEM((VS * sq, 128), jnp.float32)],
        compiler_params=pltpu.CompilerParams(vmem_limit_bytes=62 << 20),
        cost_estimate=pl.CostEstimate(
            flops=nb * 300000000, bytes_accessed=2 * x.size, transcendentals=0
        ),
        name="combine",
    )(x, *([] if out is None else [out]))


def contract(comb, pos, pieces, place, rr, cc, lo, name):
    nb = comb.shape[0]
    width = NA if lo == 0 else PAIRS - NA
    nt = width if width % 256 else width // 2
    npc = len(pieces)

    def kernel(pos_ref, x_ref, *refs):
        p_refs, (r_ref, c_ref, o_ref, w_ref) = refs[:npc], refs[npc:]
        q, n = pl.program_id(0), pl.program_id(1)

        @pl.when(n == 0)
        def _():
            place(p_refs, w_ref, q, pos_ref[0], pos_ref[1])

        cols = pl.ds(pl.multiple_of(n * nt, nt), nt)
        x = x_ref[...].reshape(nb * ROWS, PAIRS)
        acc = jnp.dot(x, w_ref[:, cols], preferred_element_type=jnp.float32)
        for m in range(nb):
            gap = r_ref[m] + c_ref[m]
            o_ref[m] = (acc[ROWS * m : ROWS * m + ROWS] / gap).astype(jnp.bfloat16)

    vmem = pl.BlockSpec(memory_space=pltpu.VMEM)
    return pl.pallas_call(
        kernel,
        grid=(2, width // nt),
        in_specs=[
            pl.BlockSpec(memory_space=pltpu.SMEM),
            pl.BlockSpec((nb, None, ROWS, PAIRS), lambda q, n: (0, q, 0, 0)),
        ]
        + [vmem] * npc
        + [
            pl.BlockSpec((None, nb, ROWS, 1), lambda q, n: (q, 0, 0, 0)),
            pl.BlockSpec((None, nb, 1, nt), lambda q, n: (q, 0, 0, n)),
        ],
        out_specs=pl.BlockSpec((nb, None, ROWS, nt), lambda q, n: (0, q, 0, n)),
        out_shape=jax.ShapeDtypeStruct((nb, 2, ROWS, width), jnp.bfloat16),
        scratch_shapes=[pltpu.VMEM((PAIRS, width), jnp.bfloat16)],
        compiler_params=pltpu.CompilerParams(vmem_limit_bytes=VMEM),
        cost_estimate=pl.CostEstimate(
            flops=PAIRS * width, bytes_accessed=PAIRS, transcendentals=0
        ),
        name=name,
    )(pos, comb, *pieces, rr, cc[..., lo : lo + width])


def place_a(p_refs, w_ref, q, y, z):
    for s in range(8):
        src = lax.rem(z + s, 8)

        @pl.when(lax.div(src, 4) == q)
        def _():
            for e in range(4):
                k = lax.rem(y + e, 4) * 4 + lax.rem(src, 4)
                w_ref[pl.ds(pl.multiple_of(k * NV, NV), NV), :] = p_refs[s][e]


def place_b(p_refs, w_ref, q, y, z):
    for k in range(16):
        w_ref[k * NV : k * NV + NV, :] = p_refs[0][q * 4 + k % 4, k // 4]


def merge(part, lo, out, name):
    nb, width = part.shape[0], part.shape[-1]

    def kernel(v_ref, *refs):
        o_ref, sem = refs[-2:]
        copies = [
            pltpu.make_async_copy(
                v_ref.at[e, q], o_ref.at[q, e, :, lo : lo + width], sem.at[q * nb + e]
            )
            for q in range(2)
            for e in range(nb)
        ]
        for copy in copies:
            copy.start()
        for copy in copies:
            copy.wait()

    anywhere = pl.BlockSpec(memory_space=pl.ANY)
    return pl.pallas_call(
        kernel,
        in_specs=[anywhere] * (1 if out is None else 2),
        out_specs=anywhere,
        out_shape=jax.ShapeDtypeStruct((2, nb, ROWS, PAIRS), jnp.bfloat16),
        input_output_aliases={} if out is None else {1: 0},
        scratch_shapes=[pltpu.SemaphoreType.DMA((2 * nb,))],
        compiler_params=pltpu.CompilerParams(vmem_limit_bytes=VMEM),
        name=name,
    )(part, *([] if out is None else [out]))


def y_permute(v, s):
    return lax.ppermute(v, "y", [(i, (i + s) % 4) for i in range(4)])


def z_permute(v, s):
    return lax.ppermute(v, RING, [(i, (i + s) % 8) for i in range(8)])


def tie(*vs):
    return lax.optimization_barrier(vs)


def gather_w(own, blocks):
    a, b = own[:, :NA], own[:, NA:]
    rest = lax.all_gather(b, RING + ("y",), axis=0).reshape(8, 4, NV, PAIRS - NA)
    col = jnp.stack([a, y_permute(a, -1), y_permute(a, 2), y_permute(a, 1)])
    col, blocks = tie(col, blocks)
    up, down = [col], [col]
    for s in range(3):
        up.append(z_permute(up[-1], 1))
        down.append(z_permute(down[-1], -1))
    far = jnp.concatenate([z_permute(up[3][:2], 1), z_permute(down[3][2:], -1)])
    return [col, down[1], down[2], down[3], far, up[3], up[2], up[1]], [rest], blocks


def per_device(amps, wshard, occ, occj, virt, table):
    zh, x, c = lax.axis_index("zh"), lax.axis_index("x"), lax.axis_index("c")
    y, zl = lax.axis_index("y"), lax.axis_index("zl")
    pos = jnp.stack([y, zh * 4 + zl]).astype(jnp.int32)

    blocks = jnp.transpose(amps[0, 0], (0, 2, 1, 3)).reshape(2, 8, ROWS, PAIRS)
    comb = combine(blocks, 0, None)
    part_a, part_b, blocks = gather_w(wshard[0], blocks)
    comb = combine(blocks, 1, comb)
    comb = lax.all_to_all(comb, ("x", "c"), split_axis=0, concat_axis=0, tiled=True)

    va = lax.dynamic_slice(virt, (0, (y * 4 + zl) * VS), (NO, VS)).reshape(2, 8, VS)
    va = lax.dynamic_index_in_dim(va, x * 2 + c, 1, False)
    occ_i = lax.dynamic_slice(occ, (zh * 8, 0), (8, NO))
    rr = (occ_i[None, :, None, :] - va[:, None, :, None]).reshape(2, 8, ROWS, 1)
    kb = lax.dynamic_slice(table[0], (zh * 8, 0), (8, NO)).reshape(8, 2, 8)
    kb = lax.dynamic_index_in_dim(kb, x * 2 + c, 2, False).T
    cc = (occj[0][None, None, :, None] - virt[kb][:, :, None, :]).reshape(2, 8, 1, PAIRS)

    out = None
    for lo, part, place, name in ((0, part_a, place_a, "_a"), (NA, part_b, place_b, "_b")):
        res = contract(comb, pos, part, place, rr, cc, lo, "contract" + name)
        res, comb = tie(res, comb)
        res = lax.all_to_all(res, ("x", "c"), split_axis=0, concat_axis=0, tiled=True)
        out = merge(res, lo, out, "merge" + name)
    out = out.reshape(NO, VS, NO, PAIRS)
    return jnp.transpose(out, (0, 2, 1, 3))[None, None]


def solution(mesh):
    fine = Mesh(mesh.devices.reshape(2, 4, 2, 4, 4), ("zh", "x", "c", "y", "zl"))
    ka, vert = ("zh", "x", "c"), ("y", "zl")
    in_specs = (P(None, ka, None, None, vert, None), P(ka, vert, None), P(), P(), P(), P())
    out_specs = P(None, ka, None, None, vert, None)
    return jax.shard_map(
        per_device, mesh=fine, in_specs=in_specs, out_specs=out_specs, check_vma=False
    )
```

```python
import jax
import jax.numpy as jnp
from jax import lax
from jax.experimental import pallas as pl
from jax.experimental.pallas import tpu as pltpu
from jax.sharding import Mesh, PartitionSpec as P

NO = 16
NV = 96
PAIRS = NO * NV
VS = 6
ROWS = VS * NO
VMEM = 62 << 20
RING = ("zh", "zl")
NA = 384


def combine(x, q, out):
    nb, sq, step = x.shape[1], NO * NO, 2

    def kernel(x_ref, *refs):
        o_ref, scr = refs[-2:]

        @pl.loop(0, step)
        def _(e):
            for a in range(VS):
                xa = x_ref[e, NO * a : NO * a + NO, :].astype(jnp.float32)
                for p in range(NO):
                    lo = a * sq + NO * p
                    scr[lo : lo + NO, 0:NV] = xa[:, NV * p : NV * p + NV]
            for a in range(VS):
                xa = x_ref[e, NO * a : NO * a + NO, :].astype(jnp.float32)
                swapped = jnp.concatenate(
                    [scr[pl.ds(a * sq + q, NO, stride=NO), :][:, :NV] for q in range(NO)], axis=1
                )
                o_ref[e, NO * a : NO * a + NO, :] = (2.0 * xa - swapped).astype(jnp.bfloat16)

    return pl.pallas_call(
        kernel,
        grid=(nb // step,),
        in_specs=[pl.BlockSpec((None, step, ROWS, PAIRS), lambda b: (q, b, 0, 0))]
        + [pl.BlockSpec(memory_space=pl.ANY)] * (out is not None),
        out_specs=pl.BlockSpec((step, None, ROWS, PAIRS), lambda b: (b, q, 0, 0)),
        out_shape=jax.ShapeDtypeStruct((nb, 2, ROWS, PAIRS), x.dtype),
        input_output_aliases={} if out is None else {1: 0},
        scratch_shapes=[pltpu.VMEM((VS * sq, 128), jnp.float32)],
        compiler_params=pltpu.CompilerParams(vmem_limit_bytes=62 << 20),
        cost_estimate=pl.CostEstimate(
            flops=nb * 300000000, bytes_accessed=2 * x.size, transcendentals=0
        ),
        name="combine",
    )(x, *([] if out is None else [out]))


def contract(comb, pos, pieces, place, rr, cc, lo, name):
    nb = comb.shape[0]
    width = NA if lo == 0 else PAIRS - NA
    nt = width
    npc = len(pieces)

    def kernel(pos_ref, x_ref, *refs):
        p_refs, (r_ref, c_ref, o_ref, w_ref) = refs[:npc], refs[npc:]
        q, n = pl.program_id(0), pl.program_id(1)

        if place is None:
            w = p_refs[0][...].reshape(PAIRS, width)
        else:

            @pl.when(n == 0)
            def _():
                place(p_refs, w_ref, q, pos_ref[0], pos_ref[1])

            w = w_ref[:, pl.ds(pl.multiple_of(n * nt, nt), nt)]


        x = x_ref[...].reshape(nb * ROWS, PAIRS)
        acc = jnp.dot(x, w, preferred_element_type=jnp.float32)
        for m in range(nb):
            gap = r_ref[m] + c_ref[m]
            o_ref[m] = (acc[ROWS * m : ROWS * m + ROWS] / gap).astype(jnp.bfloat16)

    if place is None:
        piece = pl.BlockSpec((4, 4, NV, width), lambda q, n: (0, q, 0, 0))
    else:
        piece = pl.BlockSpec(memory_space=pltpu.VMEM)
    return pl.pallas_call(
        kernel,
        grid=(2, width // nt),
        in_specs=[
            pl.BlockSpec(memory_space=pltpu.SMEM),
            pl.BlockSpec((nb, None, ROWS, PAIRS), lambda q, n: (0, q, 0, 0)),
        ]
        + [piece] * npc
        + [
            pl.BlockSpec((None, nb, ROWS, 1), lambda q, n: (q, 0, 0, 0)),
            pl.BlockSpec((None, nb, 1, nt), lambda q, n: (q, 0, 0, n)),
        ],
        out_specs=pl.BlockSpec((nb, None, ROWS, nt), lambda q, n: (0, q, 0, n)),
        out_shape=jax.ShapeDtypeStruct((nb, 2, ROWS, width), jnp.bfloat16),
        scratch_shapes=[pltpu.VMEM((PAIRS, width) if place else (16, 128), jnp.bfloat16)],
        compiler_params=pltpu.CompilerParams(vmem_limit_bytes=48 << 20),
        cost_estimate=pl.CostEstimate(
            flops=PAIRS * width, bytes_accessed=PAIRS, transcendentals=0
        ),
        name=name,
    )(pos, comb, *pieces, rr, cc[..., lo : lo + width])


def place_a(p_refs, w_ref, q, y, z):
    for s in range(8):
        src = lax.rem(z + s, 8)

        @pl.when(lax.div(src, 4) == q)
        def _():
            for e in range(4):
                k = lax.rem(y + e, 4) * 4 + lax.rem(src, 4)
                w_ref[pl.ds(pl.multiple_of(k * NV, NV), NV), :] = p_refs[s][e]


def merge(part, lo, out, name):
    nb, width = part.shape[0], part.shape[-1]

    def kernel(v_ref, *refs):
        o_ref, sem = refs[-2:]
        copies = [
            pltpu.make_async_copy(
                v_ref.at[e, q], o_ref.at[q, e, :, lo : lo + width], sem.at[q * nb + e]
            )
            for q in range(2)
            for e in range(nb)
        ]
        for copy in copies:
            copy.start()
        for copy in copies:
            copy.wait()

    anywhere = pl.BlockSpec(memory_space=pl.ANY)
    return pl.pallas_call(
        kernel,
        in_specs=[pl.BlockSpec(memory_space=pltpu.VMEM)] + [anywhere] * (out is not None),
        out_specs=anywhere,
        out_shape=jax.ShapeDtypeStruct((2, nb, ROWS, PAIRS), jnp.bfloat16),
        input_output_aliases={} if out is None else {1: 0},
        scratch_shapes=[pltpu.SemaphoreType.DMA((2 * nb,))],
        compiler_params=pltpu.CompilerParams(vmem_limit_bytes=48 << 20),
        name=name,
    )(part, *([] if out is None else [out]))


def y_permute(v, s):
    return lax.ppermute(v, "y", [(i, (i + s) % 4) for i in range(4)])


def z_permute(v, s):
    return lax.ppermute(v, RING, [(i, (i + s) % 8) for i in range(8)])


def tie(*vs):
    return lax.optimization_barrier(vs)


def gather_w(own, blocks):
    a, b = own[:, :NA], own[:, NA:]
    rest = lax.all_gather(b, ("y",) + RING, axis=0).reshape(4, 8, NV, PAIRS - NA)
    col = jnp.stack([a, y_permute(a, -1), y_permute(a, 2), y_permute(a, 1)])
    col, blocks = tie(col, blocks)
    up, down = [col], [col]
    for s in range(3):
        up.append(z_permute(up[-1], 1))
        down.append(z_permute(down[-1], -1))
    far = jnp.concatenate([z_permute(up[3][:2], 1), z_permute(down[3][2:], -1)])
    return [col, down[1], down[2], down[3], far, up[3], up[2], up[1]], [rest], blocks


def per_device(amps, wshard, occ, occj, virt, table):
    zh, x, c = lax.axis_index("zh"), lax.axis_index("x"), lax.axis_index("c")
    y, zl = lax.axis_index("y"), lax.axis_index("zl")
    pos = jnp.stack([y, zh * 4 + zl]).astype(jnp.int32)

    blocks = jnp.transpose(amps[0, 0], (0, 2, 1, 3)).reshape(2, 8, ROWS, PAIRS)
    comb = combine(blocks, 0, None)
    part_a, part_b, blocks = gather_w(wshard[0], blocks)
    comb = combine(blocks, 1, comb)
    comb = lax.all_to_all(comb, ("x", "c"), split_axis=0, concat_axis=0, tiled=True)

    va = lax.dynamic_slice(virt, (0, (y * 4 + zl) * VS), (NO, VS)).reshape(2, 8, VS)
    va = lax.dynamic_index_in_dim(va, x * 2 + c, 1, False)
    occ_i = lax.dynamic_slice(occ, (zh * 8, 0), (8, NO))
    rr = (occ_i[None, :, None, :] - va[:, None, :, None]).reshape(2, 8, ROWS, 1)
    kb = lax.dynamic_slice(table[0], (zh * 8, 0), (8, NO)).reshape(8, 2, 8)
    kb = lax.dynamic_index_in_dim(kb, x * 2 + c, 2, False).T
    cc = (occj[0][None, None, :, None] - virt[kb][:, :, None, :]).reshape(2, 8, 1, PAIRS)

    out = None
    for lo, part, place, name in ((0, part_a, place_a, "_a"), (NA, part_b, None, "_b")):
        res = contract(comb, pos, part, place, rr, cc, lo, "contract" + name)
        res, comb = tie(res, comb)
        res = lax.all_to_all(res, ("x", "c"), split_axis=0, concat_axis=0, tiled=True)
        out = merge(res, lo, out, "merge" + name)
    out = out.reshape(NO, VS, NO, PAIRS)
    return jnp.transpose(out, (0, 2, 1, 3))[None, None]


def solution(mesh):
    fine = Mesh(mesh.devices.reshape(2, 4, 2, 4, 4), ("zh", "x", "c", "y", "zl"))
    ka, vert = ("zh", "x", "c"), ("y", "zl")
    in_specs = (P(None, ka, None, None, vert, None), P(ka, vert, None), P(), P(), P(), P())
    out_specs = P(None, ka, None, None, vert, None)
    return jax.shard_map(
        per_device, mesh=fine, in_specs=in_specs, out_specs=out_specs, check_vma=False
    )
```

```python
import jax
import jax.numpy as jnp
from jax import lax
from jax.experimental import pallas as pl
from jax.experimental.pallas import tpu as pltpu
from jax.sharding import Mesh, PartitionSpec as P

NO = 16
NV = 96
PAIRS = NO * NV
VS = 6
ROWS = VS * NO
VMEM = 62 << 20
RING = ("zh", "zl")
NA = 384


def combine(x, q, out):
    nb, sq, step = x.shape[1], NO * NO, 2

    def kernel(x_ref, *refs):
        o_ref, scr = refs[-2:]

        @pl.loop(0, step)
        def _(e):
            for a in range(VS):
                xa = x_ref[e, NO * a : NO * a + NO, :].astype(jnp.float32)
                for p in range(NO):
                    lo = a * sq + NO * p
                    scr[lo : lo + NO, 0:NV] = xa[:, NV * p : NV * p + NV]
            for a in range(VS):
                xa = x_ref[e, NO * a : NO * a + NO, :].astype(jnp.float32)
                swapped = jnp.concatenate(
                    [scr[pl.ds(a * sq + q, NO, stride=NO), :][:, :NV] for q in range(NO)], axis=1
                )
                o_ref[e, NO * a : NO * a + NO, :] = (2.0 * xa - swapped).astype(jnp.bfloat16)

    return pl.pallas_call(
        kernel,
        grid=(nb // step,),
        in_specs=[pl.BlockSpec((None, step, ROWS, PAIRS), lambda b: (q, b, 0, 0))]
        + [pl.BlockSpec(memory_space=pl.ANY)] * (out is not None),
        out_specs=pl.BlockSpec((step, None, ROWS, PAIRS), lambda b: (b, q, 0, 0)),
        out_shape=jax.ShapeDtypeStruct((nb, 2, ROWS, PAIRS), x.dtype),
        input_output_aliases={} if out is None else {1: 0},
        scratch_shapes=[pltpu.VMEM((VS * sq, 128), jnp.float32)],
        compiler_params=pltpu.CompilerParams(vmem_limit_bytes=62 << 20),
        cost_estimate=pl.CostEstimate(
            flops=nb * 300000000, bytes_accessed=2 * x.size, transcendentals=0
        ),
        name="combine",
    )(x, *([] if out is None else [out]))


def contract(comb, pos, pieces, place, rr, cc, lo, name):
    nb = comb.shape[0]
    width = NA if lo == 0 else PAIRS - NA
    nt = width
    npc = len(pieces)

    def kernel(pos_ref, x_ref, *refs):
        p_refs, (r_ref, c_ref, o_ref, w_ref) = refs[:npc], refs[npc:]
        q, n = pl.program_id(0), pl.program_id(1)

        if place is None:
            w = p_refs[0][...].reshape(PAIRS, width)
        else:

            @pl.when(n == 0)
            def _():
                place(p_refs, w_ref, q, pos_ref[0], pos_ref[1])

            w = w_ref[...]

        x = x_ref[...].reshape(nb * ROWS, PAIRS)
        even = width // 256 * 256
        for left, right in ((0, even), (even, width)):
            acc = jnp.dot(x, w[:, left:right], preferred_element_type=jnp.float32)
            for m in range(nb):
                gap = r_ref[m] + c_ref[m, :, left:right]
                val = acc[ROWS * m : ROWS * m + ROWS] / gap
                o_ref[m, :, left:right] = val.astype(jnp.bfloat16)

    if place is None:
        piece = pl.BlockSpec((4, 4, NV, width), lambda q, n: (0, q, 0, 0))
    else:
        piece = pl.BlockSpec(memory_space=pltpu.VMEM)
    return pl.pallas_call(
        kernel,
        grid=(2, width // nt),
        in_specs=[
            pl.BlockSpec(memory_space=pltpu.SMEM),
            pl.BlockSpec((nb, None, ROWS, PAIRS), lambda q, n: (0, q, 0, 0)),
        ]
        + [piece] * npc
        + [
            pl.BlockSpec((None, nb, ROWS, 1), lambda q, n: (q, 0, 0, 0)),
            pl.BlockSpec((None, nb, 1, nt), lambda q, n: (q, 0, 0, n)),
        ],
        out_specs=pl.BlockSpec((nb, None, ROWS, nt), lambda q, n: (0, q, 0, n)),
        out_shape=jax.ShapeDtypeStruct((nb, 2, ROWS, width), jnp.bfloat16),
        scratch_shapes=[pltpu.VMEM((PAIRS, width) if place else (16, 128), jnp.bfloat16)],
        compiler_params=pltpu.CompilerParams(vmem_limit_bytes=48 << 20),
        cost_estimate=pl.CostEstimate(
            flops=PAIRS * width, bytes_accessed=PAIRS, transcendentals=0
        ),
        name=name,
    )(pos, comb, *pieces, rr, cc[..., lo : lo + width])


def place_a(p_refs, w_ref, q, y, z):
    for s in range(8):
        src = lax.rem(z + s, 8)

        @pl.when(lax.div(src, 4) == q)
        def _():
            for e in range(4):
                k = lax.rem(y + e, 4) * 4 + lax.rem(src, 4)
                w_ref[pl.ds(pl.multiple_of(k * NV, NV), NV), :] = p_refs[s][e]


def merge(part, lo, out, name):
    nb, width = part.shape[0], part.shape[-1]

    def kernel(v_ref, *refs):
        o_ref, sem = refs[-2:]
        copies = [
            pltpu.make_async_copy(
                v_ref.at[e, q], o_ref.at[q, e, :, lo : lo + width], sem.at[q * nb + e]
            )
            for q in range(2)
            for e in range(nb)
        ]
        for copy in copies:
            copy.start()
        for copy in copies:
            copy.wait()

    anywhere = pl.BlockSpec(memory_space=pl.ANY)
    return pl.pallas_call(
        kernel,
        in_specs=[pl.BlockSpec(memory_space=pltpu.VMEM)] + [anywhere] * (out is not None),
        out_specs=anywhere,
        out_shape=jax.ShapeDtypeStruct((2, nb, ROWS, PAIRS), jnp.bfloat16),
        input_output_aliases={} if out is None else {1: 0},
        scratch_shapes=[pltpu.SemaphoreType.DMA((2 * nb,))],
        compiler_params=pltpu.CompilerParams(vmem_limit_bytes=48 << 20),
        name=name,
    )(part, *([] if out is None else [out]))


def y_permute(v, s):
    return lax.ppermute(v, "y", [(i, (i + s) % 4) for i in range(4)])


def z_permute(v, s):
    return lax.ppermute(v, RING, [(i, (i + s) % 8) for i in range(8)])


def tie(*vs):
    return lax.optimization_barrier(vs)


def gather_w(own, blocks):
    a, b = own[:, :NA], own[:, NA:]
    rest = lax.all_gather(b, ("y",) + RING, axis=0).reshape(4, 8, NV, PAIRS - NA)
    col = jnp.stack([a, y_permute(a, -1), y_permute(a, 2), y_permute(a, 1)])
    col, blocks = tie(col, blocks)
    up, down = [col], [col]
    for s in range(3):
        up.append(z_permute(up[-1], 1))
        down.append(z_permute(down[-1], -1))
    far = jnp.concatenate([z_permute(up[3][:2], 1), z_permute(down[3][2:], -1)])
    return [col, down[1], down[2], down[3], far, up[3], up[2], up[1]], [rest], blocks


def per_device(amps, wshard, occ, occj, virt, table):
    zh, x, c = lax.axis_index("zh"), lax.axis_index("x"), lax.axis_index("c")
    y, zl = lax.axis_index("y"), lax.axis_index("zl")
    pos = jnp.stack([y, zh * 4 + zl]).astype(jnp.int32)

    blocks = jnp.transpose(amps[0, 0], (0, 2, 1, 3)).reshape(2, 8, ROWS, PAIRS)
    comb = combine(blocks, 0, None)
    part_a, part_b, blocks = gather_w(wshard[0], blocks)
    comb = combine(blocks, 1, comb)
    comb = lax.all_to_all(comb, ("x", "c"), split_axis=0, concat_axis=0, tiled=True)

    va = lax.dynamic_slice(virt, (0, (y * 4 + zl) * VS), (NO, VS)).reshape(2, 8, VS)
    va = lax.dynamic_index_in_dim(va, x * 2 + c, 1, False)
    occ_i = lax.dynamic_slice(occ, (zh * 8, 0), (8, NO))
    rr = (occ_i[None, :, None, :] - va[:, None, :, None]).reshape(2, 8, ROWS, 1)
    kb = lax.dynamic_slice(table[0], (zh * 8, 0), (8, NO)).reshape(8, 2, 8)
    kb = lax.dynamic_index_in_dim(kb, x * 2 + c, 2, False).T
    cc = (occj[0][None, None, :, None] - virt[kb][:, :, None, :]).reshape(2, 8, 1, PAIRS)

    out = None
    for lo, part, place, name in ((0, part_a, place_a, "_a"), (NA, part_b, None, "_b")):
        res = contract(comb, pos, part, place, rr, cc, lo, "contract" + name)
        res, comb = tie(res, comb)
        res = lax.all_to_all(res, ("x", "c"), split_axis=0, concat_axis=0, tiled=True)
        out = merge(res, lo, out, "merge" + name)
    out = out.reshape(NO, VS, NO, PAIRS)
    return jnp.transpose(out, (0, 2, 1, 3))[None, None]


def solution(mesh):
    fine = Mesh(mesh.devices.reshape(2, 4, 2, 4, 4), ("zh", "x", "c", "y", "zl"))
    ka, vert = ("zh", "x", "c"), ("y", "zl")
    in_specs = (P(None, ka, None, None, vert, None), P(ka, vert, None), P(), P(), P(), P())
    out_specs = P(None, ka, None, None, vert, None)
    return jax.shard_map(
        per_device, mesh=fine, in_specs=in_specs, out_specs=out_specs, check_vma=False
    )
```

```python
import jax
import jax.numpy as jnp
from jax import lax
from jax.experimental import pallas as pl
from jax.experimental.pallas import tpu as pltpu
from jax.sharding import Mesh, PartitionSpec as P

NO = 16
NV = 96
PAIRS = NO * NV
VS = 6
ROWS = VS * NO
VMEM = 62 << 20
RING = ("zh", "zl")
NA = 384


def combine(x, q, out):
    nb, sq, step = x.shape[1], NO * NO, 4

    def kernel(x_ref, *refs):
        o_ref, scr = refs[-2:]

        @pl.loop(0, step)
        def _(e):
            for a in range(VS):
                xa = x_ref[e, NO * a : NO * a + NO, :].astype(jnp.float32)
                for p in range(NO):
                    lo = a * sq + NO * p
                    scr[lo : lo + NO, 0:NV] = xa[:, NV * p : NV * p + NV]
            for a in range(VS):
                xa = x_ref[e, NO * a : NO * a + NO, :].astype(jnp.float32)
                swapped = jnp.concatenate(
                    [scr[pl.ds(a * sq + q, NO, stride=NO), :][:, :NV] for q in range(NO)], axis=1
                )
                o_ref[e, NO * a : NO * a + NO, :] = (2.0 * xa - swapped).astype(jnp.bfloat16)

    return pl.pallas_call(
        kernel,
        grid=(nb // step,),
        in_specs=[pl.BlockSpec((None, step, ROWS, PAIRS), lambda b: (q, b, 0, 0))]
        + [pl.BlockSpec(memory_space=pl.ANY)] * (out is not None),
        out_specs=pl.BlockSpec((step, None, ROWS, PAIRS), lambda b: (b, q, 0, 0)),
        out_shape=jax.ShapeDtypeStruct((nb, 2, ROWS, PAIRS), x.dtype),
        input_output_aliases={} if out is None else {1: 0},
        scratch_shapes=[pltpu.VMEM((VS * sq, 128), jnp.float32)],
        compiler_params=pltpu.CompilerParams(vmem_limit_bytes=62 << 20),
        cost_estimate=pl.CostEstimate(
            flops=nb * 300000000, bytes_accessed=2 * x.size, transcendentals=0
        ),
        name="combine",
    )(x, *([] if out is None else [out]))


def contract(comb, pos, pieces, place, rr, cc, lo, name):
    nb = comb.shape[0]
    width = NA if lo == 0 else PAIRS - NA
    nt = width
    npc = len(pieces)

    def kernel(pos_ref, x_ref, *refs):
        p_refs, (r_ref, c_ref, o_ref, w_ref) = refs[:npc], refs[npc:]
        q, n = pl.program_id(0), pl.program_id(1)

        if place is None:
            w = p_refs[0][...].reshape(PAIRS, width)
        else:

            @pl.when(n == 0)
            def _():
                place(p_refs, w_ref, q, pos_ref[0], pos_ref[1])

            w = w_ref[...]

        x = x_ref[...].reshape(nb * ROWS, PAIRS)
        even = width // 256 * 256
        for left, right in ((0, even), (even, width)):
            acc = jnp.dot(x, w[:, left:right], preferred_element_type=jnp.float32)
            for m in range(nb):
                gap = r_ref[m] + c_ref[m, :, left:right]
                val = acc[ROWS * m : ROWS * m + ROWS] / gap
                o_ref[m, :, left:right] = val.astype(jnp.bfloat16)

    if place is None:
        piece = pl.BlockSpec((4, 4, NV, width), lambda q, n: (0, q, 0, 0))
    else:
        piece = pl.BlockSpec(memory_space=pltpu.VMEM)
    return pl.pallas_call(
        kernel,
        grid=(2, width // nt),
        in_specs=[
            pl.BlockSpec(memory_space=pltpu.SMEM),
            pl.BlockSpec((nb, None, ROWS, PAIRS), lambda q, n: (0, q, 0, 0)),
        ]
        + [piece] * npc
        + [
            pl.BlockSpec((None, nb, ROWS, 1), lambda q, n: (q, 0, 0, 0)),
            pl.BlockSpec((None, nb, 1, nt), lambda q, n: (q, 0, 0, n)),
        ],
        out_specs=pl.BlockSpec((nb, None, ROWS, nt), lambda q, n: (0, q, 0, n)),
        out_shape=jax.ShapeDtypeStruct((nb, 2, ROWS, width), jnp.bfloat16),
        scratch_shapes=[pltpu.VMEM((PAIRS, width) if place else (16, 128), jnp.bfloat16)],
        compiler_params=pltpu.CompilerParams(vmem_limit_bytes=48 << 20),
        cost_estimate=pl.CostEstimate(
            flops=PAIRS * width, bytes_accessed=PAIRS, transcendentals=0
        ),
        name=name,
    )(pos, comb, *pieces, rr, cc[..., lo : lo + width])


def place_a(p_refs, w_ref, q, y, z):
    for s in range(8):
        src = lax.rem(z + s, 8)

        @pl.when(lax.div(src, 4) == q)
        def _():
            for e in range(4):
                k = lax.rem(y + e, 4) * 4 + lax.rem(src, 4)
                w_ref[pl.ds(pl.multiple_of(k * NV, NV), NV), :] = p_refs[s][e]


def merge(part, lo, out, name):
    nb, width = part.shape[0], part.shape[-1]

    def kernel(v_ref, *refs):
        o_ref, sem = refs[-2:]
        copies = [
            pltpu.make_async_copy(
                v_ref.at[e, q], o_ref.at[q, e, :, lo : lo + width], sem.at[q * nb + e]
            )
            for q in range(2)
            for e in range(nb)
        ]
        for copy in copies:
            copy.start()
        for copy in copies:
            copy.wait()

    anywhere = pl.BlockSpec(memory_space=pl.ANY)
    return pl.pallas_call(
        kernel,
        in_specs=[pl.BlockSpec(memory_space=pltpu.VMEM)] + [anywhere] * (out is not None),
        out_specs=anywhere,
        out_shape=jax.ShapeDtypeStruct((2, nb, ROWS, PAIRS), jnp.bfloat16),
        input_output_aliases={} if out is None else {1: 0},
        scratch_shapes=[pltpu.SemaphoreType.DMA((2 * nb,))],
        compiler_params=pltpu.CompilerParams(vmem_limit_bytes=48 << 20),
        name=name,
    )(part, *([] if out is None else [out]))


def y_permute(v, s):
    return lax.ppermute(v, "y", [(i, (i + s) % 4) for i in range(4)])


def z_permute(v, s):
    return lax.ppermute(v, RING, [(i, (i + s) % 8) for i in range(8)])


def tie(*vs):
    return lax.optimization_barrier(vs)


def gather_w(own, blocks):
    a, b = own[:, :NA], own[:, NA:]
    rest = lax.all_gather(b, ("y",) + RING, axis=0).reshape(4, 8, NV, PAIRS - NA)
    col = jnp.stack([a, y_permute(a, -1), y_permute(a, 2), y_permute(a, 1)])
    col, blocks = tie(col, blocks)
    up, down = [col], [col]
    for s in range(3):
        up.append(z_permute(up[-1], 1))
        down.append(z_permute(down[-1], -1))
    far = jnp.concatenate([z_permute(up[3][:2], 1), z_permute(down[3][2:], -1)])
    return [col, down[1], down[2], down[3], far, up[3], up[2], up[1]], [rest], blocks


def per_device(amps, wshard, occ, occj, virt, table):
    zh, x, c = lax.axis_index("zh"), lax.axis_index("x"), lax.axis_index("c")
    y, zl = lax.axis_index("y"), lax.axis_index("zl")
    pos = jnp.stack([y, zh * 4 + zl]).astype(jnp.int32)

    blocks = jnp.transpose(amps[0, 0], (0, 2, 1, 3)).reshape(2, 8, ROWS, PAIRS)
    comb = combine(blocks, 0, None)
    part_a, part_b, blocks = gather_w(wshard[0], blocks)
    comb = combine(blocks, 1, comb)
    comb = lax.all_to_all(comb, ("x", "c"), split_axis=0, concat_axis=0, tiled=True)

    va = lax.dynamic_slice(virt, (0, (y * 4 + zl) * VS), (NO, VS)).reshape(2, 8, VS)
    va = lax.dynamic_index_in_dim(va, x * 2 + c, 1, False)
    occ_i = lax.dynamic_slice(occ, (zh * 8, 0), (8, NO))
    rr = (occ_i[None, :, None, :] - va[:, None, :, None]).reshape(2, 8, ROWS, 1)
    kb = lax.dynamic_slice(table[0], (zh * 8, 0), (8, NO)).reshape(8, 2, 8)
    kb = lax.dynamic_index_in_dim(kb, x * 2 + c, 2, False).T
    cc = (occj[0][None, None, :, None] - virt[kb][:, :, None, :]).reshape(2, 8, 1, PAIRS)

    out = None
    for lo, part, place, name in ((0, part_a, place_a, "_a"), (NA, part_b, None, "_b")):
        res = contract(comb, pos, part, place, rr, cc, lo, "contract" + name)
        res, comb = tie(res, comb)
        res = lax.all_to_all(res, ("x", "c"), split_axis=0, concat_axis=0, tiled=True)
        out = merge(res, lo, out, "merge" + name)
    out = out.reshape(NO, VS, NO, PAIRS)
    return jnp.transpose(out, (0, 2, 1, 3))[None, None]


def solution(mesh):
    fine = Mesh(mesh.devices.reshape(2, 4, 2, 4, 4), ("zh", "x", "c", "y", "zl"))
    ka, vert = ("zh", "x", "c"), ("y", "zl")
    in_specs = (P(None, ka, None, None, vert, None), P(ka, vert, None), P(), P(), P(), P())
    out_specs = P(None, ka, None, None, vert, None)
    return jax.shard_map(
        per_device, mesh=fine, in_specs=in_specs, out_specs=out_specs, check_vma=False
    )
```
